32 devices in a mesh: dp: 8 (over y, x, core), tensor: 4 (over z).
Axes of the slice: x: 2, y: 2, z: 4, core: 2. Of those that a mesh axis runs over, the one named last changes fastest.
Arguments:
- tokens: bfloat16 [16384, 1024], P(('dp', 'tensor')), may hold values from -6 to 6
- out_grad: bfloat16 [16384, 1024], P(('dp', 'tensor')), may hold values from -6 to 6
- seq_lengths: int32 [8, 8], P('dp'), may hold values from 1 to 1024, 2048 in all within a row
- master_qkv: float32 [1024, 3, 1024], P('dp', None, 'tensor'), may hold values from -0.1875 to 0.1875
- first_qkv: float32 [1024, 3, 1024], P('dp', None, 'tensor'), may hold values from -24 to 24
- second_qkv: float32 [1024, 3, 1024], P('dp', None, 'tensor'), may hold values from 1.47456 to 5.89824
- master_mix: float32 [1024, 1024], P('dp', 'tensor'), may hold values from -0.1875 to 0.1875
- first_mix: float32 [1024, 1024], P('dp', 'tensor'), may hold values from -80 to 80
- second_mix: float32 [1024, 1024], P('dp', 'tensor'), may hold values from 16.384 to 65.536
- master_up: float32 [1024, 4096], P('dp', 'tensor'), may hold values from -0.35625 to 0.35625
- first_up: float32 [1024, 4096], P('dp', 'tensor'), may hold values from -24 to 24
- second_up: float32 [1024, 4096], P('dp', 'tensor'), may hold values from 1.47456 to 5.89824
- master_down: float32 [1024, 4096], P('dp', 'tensor'), may hold values from -0.09375 to 0.09375
- first_down: float32 [1024, 4096], P('dp', 'tensor'), may hold values from -80 to 80
- second_down: float32 [1024, 4096], P('dp', 'tensor'), may hold values from 16.384 to 65.536
- master_norms: float32 [6, 1024], replicated, may hold values from -1.2 to 2.02
- first_norms: float32 [6, 1024], replicated, may hold values from -80 to 80
- second_norms: float32 [6, 1024], replicated, may hold values from 16.384 to 65.536
- master_midnorm: float32 [2, 4096], replicated, may hold values from -1.2 to 2.02
- first_midnorm: float32 [2, 4096], replicated, may hold values from -40 to 40
- second_midnorm: float32 [2, 4096], replicated, may hold values from 4.096 to 16.384
- master_heads: float32 [16], replicated, may hold values from 0.5 to 2
- first_heads: float32 [16], replicated, may hold values from -640 to 640
- second_heads: float32 [16], replicated, may hold values from 1048.576 to 4194.304
Outputs:
- layer_out: bfloat16 [16384, 1024], P(('dp', 'tensor'))
- input_grad: float32 [16384, 1024], P(('dp', 'tensor'))
- updated_qkv: float32 [1024, 3, 1024], P('dp', None, 'tensor')
- moment_qkv: float32 [1024, 3, 1024], P('dp', None, 'tensor')
- square_qkv: float32 [1024, 3, 1024], P('dp', None, 'tensor')
- updated_mix: float32 [1024, 1024], P('dp', 'tensor')
- moment_mix: float32 [1024, 1024], P('dp', 'tensor')
- square_mix: float32 [1024, 1024], P('dp', 'tensor')
- updated_up: float32 [1024, 4096], P('dp', 'tensor')
- moment_up: float32 [1024, 4096], P('dp', 'tensor')
- square_up: float32 [1024, 4096], P('dp', 'tensor')
- updated_down: float32 [1024, 4096], P('dp', 'tensor')
- moment_down: float32 [1024, 4096], P('dp', 'tensor')
- square_down: float32 [1024, 4096], P('dp', 'tensor')
- updated_norms: float32 [6, 1024], replicated
- moment_norms: float32 [6, 1024], replicated
- square_norms: float32 [6, 1024], replicated
- updated_midnorm: float32 [2, 4096], replicated
- moment_midnorm: float32 [2, 4096], replicated
- square_midnorm: float32 [2, 4096], replicated
- updated_heads: float32 [16], replicated
- moment_heads: float32 [16], replicated
- square_heads: float32 [16], replicated
The draws below stay inside these ranges and needn't reach their ends.
Inputs may be any that keep to these rules, and one draw needn't show every extreme that they name: `seq_lengths`: row g lists, in order, the lengths of the 8 sequences packed into data group g's 2048 token slots; each row sums to 2048 and holds one sequence of exactly 1024 tokens.
All inputs are finite; a program needn't handle non-finite values.
Results may differ from the reference program's by a relative error of at most 0.012.
The reference program's roundings to bfloat16 on the way count: a program that leaves them out, or rounds other values in their place, can miss the bound.
Values may be sent and summed in bfloat16 or wider, within the bound.
No kernel may reach another device: no remote copies, remote signals or barrier semaphores. Data moves between devices by JAX's collectives and lax.ppermute only.
A program may use at most 192 MiB of HBM per device.

```python
import math
import jax
import jax.numpy as jnp
import numpy as np
from jax import lax

D = 1024
HEADS = 16
HEAD_DIM = 64
FF = 4096
TOK_G = 2048
SLOTS = 8
QBLOCK = 512
STEP = 10
LONGEST = 1024
TOKENS = 16384
N_DP = 8


def draw_master_up(key, part):
    first, second = jax.random.split(jax.random.fold_in(key, 11))
    column = jnp.arange(FF, dtype=jnp.float32) / (FF - 1)
    base = jax.random.truncated_normal(first, -4.0, 4.0, (D, FF), jnp.float32)
    ramp = jnp.exp(column * math.log(2.0))
    rough = jnp.exp(jax.random.uniform(second, (1, FF), jnp.float32, -0.35, 0.35))
    return base * ramp[None, :] * rough * D ** (-0.5)


def gains_biases(key, rows, width):
    first, second = jax.random.split(key)
    gains = jnp.exp(jax.random.uniform(first, (rows, width), jnp.float32, -0.7, 0.7))
    biases = 0.3 * jax.random.truncated_normal(second, -4.0, 4.0, (rows, width), jnp.float32)
    return jnp.stack([gains, biases], 1).reshape(2 * rows, width)


def draw_master_norms(key, part):
    return gains_biases(jax.random.fold_in(key, 23), 3, D)


def draw_master_midnorm(key, part):
    return gains_biases(jax.random.fold_in(key, 37), 1, FF)


def levels(rng, dims, shards, least, top_value):
    loudness = 1.0
    for axis_at, blocks in shards:
        draws = jax.random.uniform(jax.random.fold_in(jax.random.fold_in(rng, 6), axis_at), (blocks,), jnp.float32, least / len(shards), top_value / len(shards))
        loudness = loudness * jnp.repeat(jnp.exp(draws), dims[axis_at] // blocks).reshape((-1,) + (1,) * (len(dims) - 1 - axis_at))
    return loudness


def profile(count, total, most, lean):
    portions = [(1 << 20) // math.isqrt(grade ** lean) + 1 for grade in range(2, count + 1)]
    spare, counts = total - most - (count - 1), [1] * (count - 1)
    while spare > 0:
        movable = [i for i in range(count - 1) if counts[i] < most]
        mass, left = sum([portions[i] for i in movable]), spare
        for i in movable:
            extra = min(most - counts[i], max(1, left * portions[i] // mass), spare)
            counts[i] = counts[i] + extra
            spare = spare - extra
    return np.array([most] + counts)


def uneven(key, amount, total, bound, lean):
    if amount == 2:
        one = jax.random.randint(key, (), max(1, total - bound), min(bound, total - 1) + 1)
        return jnp.stack([one, total - one])
    sizes = jnp.asarray(profile(amount, total, bound, lean), jnp.int32)
    pairs = (amount - 1) // 2
    donor, taker = sizes[1:1 + 2 * pairs:2], sizes[2:2 + 2 * pairs:2]
    margin = jnp.minimum(donor - 1, bound - taker)
    passed = jax.random.randint(jax.random.fold_in(key, 1), (pairs,), 0, 1 << 20) % (margin + 1)
    sizes = sizes.at[1:1 + 2 * pairs:2].set(donor - passed).at[2:2 + 2 * pairs:2].set(taker + passed)
    return sizes[jax.random.permutation(jax.random.fold_in(key, 2), amount)]


def gaussian(stream_key, shape, scale, bound, shards=(), kind=jnp.bfloat16):
    values = scale * jax.random.normal(stream_key, shape, jnp.float32)
    if shards:
        values = values * levels(stream_key, shape, shards, -0.22, 0.18)
    return jnp.clip(values, -bound, bound).astype(kind)


def setup_inputs(seed: int = 0) -> dict:
    key_of = jax.random.split(jax.random.key(seed), 25)
    return {
        "tokens": gaussian(key_of[0], (TOKENS, D), 1.0, 6.0, ((0, 32),)),
        "out_grad": gaussian(key_of[1], (TOKENS, D), 1.0, 6.0, ((0, 32),)),
        "seq_lengths": jax.vmap(lambda own: uneven(own, SLOTS, TOK_G, LONGEST, 2))(jax.random.split(key_of[2], N_DP)).reshape((N_DP, SLOTS)).astype(jnp.int32),
        "master_qkv": gaussian(key_of[3], (D, 3, D), D ** -0.5, 0.1875, ((0, 8), (2, 4)), jnp.float32),
        "first_qkv": gaussian(key_of[4], (D, 3, D), (0.033 * TOKENS ** 0.5), 24.0, ((0, 8), (2, 4)), jnp.float32),
        "second_qkv": jnp.clip(jnp.exp(math.log(5.89824) - 1.3862944 * jax.random.uniform(key_of[5], (D, 3, D), jnp.float32) ** levels(key_of[5], (D, 3, D), ((0, 8), (2, 4)), -0.2, 0.2)), 1.47456, 5.89824),
        "master_mix": gaussian(key_of[6], (D, D), D ** -0.5, 0.1875, ((0, 8), (1, 4)), jnp.float32),
        "first_mix": gaussian(key_of[7], (D, D), (0.11 * TOKENS ** 0.5), 80.0, ((0, 8), (1, 4)), jnp.float32),
        "second_mix": jnp.clip(jnp.exp(math.log(65.536) - 1.3862944 * jax.random.uniform(key_of[8], (D, D), jnp.float32) ** levels(key_of[8], (D, D), ((0, 8), (1, 4)), -0.2, 0.2)), 16.384, 65.536),
        "master_up": draw_master_up(jax.random.fold_in(key_of[24], 71), 0),
        "first_up": gaussian(key_of[10], (D, FF), (0.033 * TOKENS ** 0.5), 24.0, ((0, 8), (1, 4)), jnp.float32),
        "second_up": jnp.clip(jnp.exp(math.log(5.89824) - 1.3862944 * jax.random.uniform(key_of[11], (D, FF), jnp.float32) ** levels(key_of[11], (D, FF), ((0, 8), (1, 4)), -0.2, 0.2)), 1.47456, 5.89824),
        "master_down": gaussian(key_of[12], (D, FF), FF ** -0.5, 0.09375, ((0, 8), (1, 4)), jnp.float32),
        "first_down": gaussian(key_of[13], (D, FF), (0.11 * TOKENS ** 0.5), 80.0, ((0, 8), (1, 4)), jnp.float32),
        "second_down": jnp.clip(jnp.exp(math.log(65.536) - 1.3862944 * jax.random.uniform(key_of[14], (D, FF), jnp.float32) ** levels(key_of[14], (D, FF), ((0, 8), (1, 4)), -0.2, 0.2)), 16.384, 65.536),
        "master_norms": draw_master_norms(jax.random.fold_in(key_of[24], 71), 0),
        "first_norms": gaussian(key_of[16], (6, D), (0.11 * TOKENS ** 0.5), 80.0, (), jnp.float32),
        "second_norms": jnp.clip(jnp.exp(jax.random.uniform(key_of[17], (6, D), jnp.float32, math.log(16.384), math.log(65.536))), 16.384, 65.536),
        "master_midnorm": draw_master_midnorm(jax.random.fold_in(key_of[24], 71), 0),
        "first_midnorm": gaussian(key_of[19], (2, FF), (0.055 * TOKENS ** 0.5), 40.0, (), jnp.float32),
        "second_midnorm": jnp.clip(jnp.exp(jax.random.uniform(key_of[20], (2, FF), jnp.float32, math.log(4.096), math.log(16.384))), 4.096, 16.384),
        "master_heads": jnp.clip(jnp.exp(jax.random.uniform(key_of[21], (HEADS,), jnp.float32, math.log(0.5), math.log(2.0))), 0.5, 2.0),
        "first_heads": gaussian(key_of[22], (HEADS,), (0.9 * TOKENS ** 0.5), 640.0, (), jnp.float32),
        "second_heads": jnp.clip(jnp.exp(jax.random.uniform(key_of[23], (HEADS,), jnp.float32, math.log(1048.576), math.log(4194.304))), 1048.576, 4194.304),
    }


highest = lax.Precision.HIGHEST
eps_norm = 1e-05
beta_one = 0.9
beta_two = 0.999
eps_adam = 1e-08
rate_matrix = 0.02
rate_vector = 0.2
decay_matrix = 0.1

@jax.custom_vjp
def low(v):
    return lax.optimization_barrier(v.astype(jnp.bfloat16)).astype(jnp.float32)

@jax.custom_vjp
def low_back(v):
    return v

def low_keep(v):
    return (low(v), None)

def low_pass(kept, grad):
    return (grad,)

def back_keep(v):
    return (v, None)

def back_low(kept, grad):
    return (low(grad),)
low.defvjp(low_keep, low_pass)
low_back.defvjp(back_keep, back_low)

def layer_norm(values, gain, bias):
    mean_row = lax.optimization_barrier(jnp.mean(values, -1, keepdims=True))
    centred = values - mean_row
    spread = lax.optimization_barrier(jnp.mean(centred * centred, -1, keepdims=True))
    return centred * lax.rsqrt(spread + eps_norm) * gain + bias

def mid_norm(values, gain, bias):
    mean_row = lax.optimization_barrier(jnp.mean(values, -1, keepdims=True))
    spread = lax.optimization_barrier(jnp.mean(values * values, -1, keepdims=True)) - mean_row * mean_row
    return (values - mean_row) * lax.rsqrt(spread + eps_norm) * gain + bias

def attend_group(packed, segment_ids):
    queries = packed[:, 0]
    padding = jnp.zeros((LONGEST, HEADS, HEAD_DIM), jnp.float32)
    keys_pad = jnp.concatenate([padding, packed[:, 1]], 0)
    values_pad = jnp.concatenate([padding, packed[:, 2]], 0)
    segment_pad = jnp.concatenate([jnp.full((LONGEST,), -1, jnp.int32), segment_ids], 0)

    def one_block(index):
        start = (index * QBLOCK).astype(jnp.int32)
        query_block = lax.dynamic_slice_in_dim(queries, start, QBLOCK, 0)
        key_block = lax.dynamic_slice_in_dim(keys_pad, start, LONGEST + QBLOCK, 0)
        value_block = lax.dynamic_slice_in_dim(values_pad, start, LONGEST + QBLOCK, 0)
        query_pos = start + jnp.arange(QBLOCK, dtype=jnp.int32)
        key_pos = start - LONGEST + jnp.arange(LONGEST + QBLOCK, dtype=jnp.int32)
        query_seg = lax.dynamic_slice_in_dim(segment_ids, start, QBLOCK, 0)
        key_seg = lax.dynamic_slice_in_dim(segment_pad, start, LONGEST + QBLOCK, 0)
        valid = (key_pos[None, :] <= query_pos[:, None]) & (key_seg[None, :] == query_seg[:, None])
        scores = low_back(jnp.einsum('qhd,khd->hqk', query_block, key_block, precision=highest) * HEAD_DIM ** (-0.5))
        scores = jnp.where(valid[None], scores, -1e+30)
        peak = lax.optimization_barrier(jnp.max(scores, 2, keepdims=True))
        raised = jnp.exp(scores - peak)
        shares = raised / lax.optimization_barrier(jnp.sum(raised, 2, keepdims=True))
        return jnp.einsum('hqk,khd->qhd', low(shares), value_block, precision=highest)
    blocks = lax.map(jax.checkpoint(one_block), jnp.arange(TOK_G // QBLOCK, dtype=jnp.int32))
    return blocks.reshape(TOK_G, HEADS, HEAD_DIM)

def group_forward(params, x_group, lengths):
    w_qkv, w_mix, w_up, w_down, norms, midnorm, heads = params
    ends = jnp.cumsum(lengths).astype(jnp.int32)
    places = jnp.arange(TOK_G, dtype=jnp.int32)
    segment_ids = lax.optimization_barrier(jnp.sum((places[:, None] >= ends[None, :]).astype(jnp.int32), 1)).astype(jnp.int32)
    normed_one = low(layer_norm(x_group, norms[0], norms[1]))
    packed = low_back(low(jnp.dot(normed_one, w_qkv.reshape(D, 3 * D), precision=highest)))
    attended = low_back(attend_group(packed.reshape(TOK_G, 3, HEADS, HEAD_DIM), segment_ids))
    scaled = low((attended * heads[None, :, None]).reshape(TOK_G, D))
    mixed = low_back(jnp.dot(scaled, w_mix.T, precision=highest))
    hidden = x_group + layer_norm(mixed, norms[2], norms[3])
    normed_three = low(layer_norm(hidden, norms[4], norms[5]))
    upper = low_back(jnp.dot(normed_three, w_up, precision=highest))
    reshaped = low(mid_norm(jax.nn.gelu(upper, approximate=False), midnorm[0], midnorm[1]))
    return hidden + jnp.dot(reshaped, w_down.T, precision=highest)

def adam_update(master, first, second, grad, rate, decay):
    moment = beta_one * first + (1.0 - beta_one) * grad
    square = beta_two * second + (1.0 - beta_two) * grad * grad
    step_size = moment / (1.0 - beta_one ** STEP) / (jnp.sqrt(square / (1.0 - beta_two ** STEP)) + eps_adam)
    updated = master - rate * (step_size + decay * master)
    return (updated, moment, square)

def reference(tokens, out_grad, seq_lengths, master_qkv, first_qkv, second_qkv, master_mix, first_mix, second_mix, master_up, first_up, second_up, master_down, first_down, second_down, master_norms, first_norms, second_norms, master_midnorm, first_midnorm, second_midnorm, master_heads, first_heads, second_heads):

    def forward(inputs, w_qkv, w_mix, w_up, w_down, norms, midnorm, heads):
        params = (low(w_qkv), low(w_mix), low(w_up), low(w_down), norms, midnorm, heads)
        grouped = inputs.reshape(N_DP, TOK_G, D)
        checked = jax.checkpoint(group_forward)

        def per_group(pair):
            return checked(params, pair[0], pair[1])
        return lax.map(per_group, (grouped, seq_lengths)).reshape(TOKENS, D)
    result, pullback = jax.vjp(forward, tokens.astype(jnp.float32), master_qkv, master_mix, master_up, master_down, master_norms, master_midnorm, master_heads)
    grads = pullback(out_grad.astype(jnp.float32))
    new_qkv = adam_update(master_qkv, first_qkv, second_qkv, grads[1], rate_matrix, decay_matrix)
    new_mix = adam_update(master_mix, first_mix, second_mix, grads[2], rate_matrix, decay_matrix)
    new_up = adam_update(master_up, first_up, second_up, grads[3], rate_matrix, decay_matrix)
    new_down = adam_update(master_down, first_down, second_down, grads[4], rate_matrix, decay_matrix)
    new_norms = adam_update(master_norms, first_norms, second_norms, grads[5], rate_vector, 0.0)
    new_midnorm = adam_update(master_midnorm, first_midnorm, second_midnorm, grads[6], rate_vector, 0.0)
    new_heads = adam_update(master_heads, first_heads, second_heads, grads[7], rate_vector, 0.0)
    return (result.astype(jnp.bfloat16), grads[0], new_qkv[0], new_qkv[1], new_qkv[2], new_mix[0], new_mix[1], new_mix[2], new_up[0], new_up[1], new_up[2], new_down[0], new_down[1], new_down[2], new_norms[0], new_norms[1], new_norms[2], new_midnorm[0], new_midnorm[1], new_midnorm[2], new_heads[0], new_heads[1], new_heads[2])
```

```python
import functools
import math

import jax
import jax.numpy as jnp
from jax import lax
from jax.experimental import pallas as pl
from jax.experimental.pallas import tpu as pltpu
from jax.sharding import PartitionSpec as P

HEADS = 16
HEAD_DIM = 64
FF = 4096
STEP = 10
LONGEST = 1024

eps_norm = 1e-05
beta_one = 0.9
beta_two = 0.999
eps_adam = 1e-08
rate_matrix = 0.02
rate_vector = 0.2
decay_matrix = 0.1
blocked = -1e30

KEYS = 256
BF = jnp.bfloat16
F32 = jnp.float32


def dot_nn(a, b):
    return lax.dot_general(a, b, (((1,), (0,)), ((), ())), preferred_element_type=F32)


def dot_nt(a, b):
    return lax.dot_general(a, b, (((1,), (1,)), ((), ())), preferred_element_type=F32)


def dot_tn(a, b):
    return lax.dot_general(a, b, (((0,), (0,)), ((), ())), preferred_element_type=F32)


def norm_forward(values, gain, bias):
    mean_row = jnp.mean(values, -1, keepdims=True)
    centred = values - mean_row
    spread = jnp.mean(centred * centred, -1, keepdims=True)
    scale_row = lax.rsqrt(spread + eps_norm)
    normal = centred * scale_row
    return (normal * gain + bias, normal, scale_row)


def norm_backward(grad_out, normal, scale_row, gain):
    grad_normal = grad_out * gain
    first_term = jnp.mean(grad_normal, -1, keepdims=True)
    second_term = jnp.mean(grad_normal * normal, -1, keepdims=True)
    grad_in = scale_row * (grad_normal - first_term - normal * second_term)
    return (grad_in, jnp.sum(grad_out * normal, 0), jnp.sum(grad_out, 0))


def gelu_exact(values):
    return jax.nn.gelu(values, approximate=False)


def adam_update(master, first, second, grad, rate, decay):
    moment = beta_one * first + (1.0 - beta_one) * grad
    square = beta_two * second + (1.0 - beta_two) * grad * grad
    step_size = (
        moment / (1.0 - beta_one**STEP) / (jnp.sqrt(square / (1.0 - beta_two**STEP)) + eps_adam)
    )
    updated = master - rate * (step_size + decay * master)
    return (updated, moment, square)


LOG2E = 1.4426950408889634


def _halves(ref_value):
    lane = lax.broadcasted_iota(jnp.int32, ref_value.shape, 1)
    zero = jnp.zeros_like(ref_value)
    return (jnp.where(lane < HEAD_DIM, ref_value, zero), jnp.where(lane >= HEAD_DIM, ref_value, zero))


def _scores(k_chunk, q_half, base, starts, places):
    s = dot_nt(k_chunk, q_half) * (LOG2E * HEAD_DIM ** (-0.5))
    key = base + lax.broadcasted_iota(jnp.int32, s.shape, 0)
    return jnp.where((key >= starts) & (key <= places), s, blocked)


def attend_forward_kernel(rows, halo, lows, q_ref, k_ref, v_ref, starts_ref, out_ref, lse_ref, vt_ref):
    window = rows + halo
    block = min(256, rows)
    vt_ref[...] = v_ref[...].T
    for b in range(rows // block):
        q = q_ref[pl.ds(b * block, block), :]
        halves = _halves(q)
        starts = starts_ref[:, pl.ds(b * block, block)]
        places = halo + b * block + lax.broadcasted_iota(jnp.int32, (1, block), 1)

        def step(c, carry):
            base = pl.multiple_of(c * KEYS, KEYS)
            k_chunk = k_ref[pl.ds(base, KEYS), :]
            new = []
            for h in range(2):
                peak, total, acc = carry[3 * h : 3 * h + 3]
                s = _scores(k_chunk, halves[h], base, starts, places)
                peak_new = jnp.maximum(peak, jnp.max(s, 0, keepdims=True))
                fade = jnp.exp2(peak - peak_new)
                raised = jnp.exp2(s - peak_new)
                total = total * fade + jnp.sum(raised, 0, keepdims=True)
                vt = vt_ref[h * HEAD_DIM : (h + 1) * HEAD_DIM, pl.ds(base, KEYS)]
                acc = acc * fade + dot_nn(vt, raised.astype(BF))
                new += [peak_new, total, acc]
            return tuple(new)

        zero = (
            jnp.full((1, block), blocked, F32),
            jnp.zeros((1, block), F32),
            jnp.zeros((HEAD_DIM, block), F32),
        )
        last = -(-(halo + (b + 1) * block) // KEYS)
        got = lax.fori_loop(lows[b], last, step, zero + zero)
        for h in range(2):
            peak, total, acc = got[3 * h : 3 * h + 3]
            out_ref[h * HEAD_DIM : (h + 1) * HEAD_DIM, pl.ds(b * block, block)] = acc / total
            lse_ref[0, h : h + 1, pl.ds(b * block, block)] = peak + jnp.log2(total)


def attend_forward(q, kv, starts, lows):
    rows, window = q.shape[0], kv.shape[0]
    halo = window - rows
    pairs = q.shape[1] // 128

    def kernel(lows_ref, *refs):
        attend_forward_kernel(rows, halo, lows_ref, *refs)

    return pl.pallas_call(
        kernel,
        grid_spec=pltpu.PrefetchScalarGridSpec(
            num_scalar_prefetch=1,
            grid=(pairs,),
            in_specs=[
                pl.BlockSpec((rows, 128), lambda p, lows: (0, p)),
                pl.BlockSpec((window, 128), lambda p, lows: (0, p)),
                pl.BlockSpec((window, 128), lambda p, lows: (0, pairs + p)),
                pl.BlockSpec((1, rows), lambda p, lows: (0, 0)),
            ],
            out_specs=[
                pl.BlockSpec((128, rows), lambda p, lows: (p, 0)),
                pl.BlockSpec((1, 2, rows), lambda p, lows: (p, 0, 0)),
            ],
            scratch_shapes=[pltpu.VMEM((128, window), BF)],
        ),
        out_shape=[
            jax.ShapeDtypeStruct((q.shape[1], rows), F32),
            jax.ShapeDtypeStruct((pairs, 2, rows), F32),
        ],
        cost_estimate=pl.CostEstimate(
            flops=4 * rows * window * q.shape[1], bytes_accessed=16 << 20, transcendentals=0
        ),
        compiler_params=pltpu.CompilerParams(vmem_limit_bytes=40 << 20),
    )(lows, q, kv, kv, starts)


def attend_backward_kernel(
    rows, halo, lows, q_ref, k_ref, v_ref, g_ref, out_ref, lse_ref, starts_ref,
    gq_ref, gkv_ref, kt_ref, gk_acc, gv_acc,
):
    block = min(256, rows)
    kt_ref[...] = k_ref[...].T
    gk_acc[...] = jnp.zeros_like(gk_acc)
    gv_acc[...] = jnp.zeros_like(gv_acc)
    scale = HEAD_DIM ** (-0.5)
    for b in range(rows // block):
        span = pl.ds(b * block, block)
        q = q_ref[span, :]
        g = g_ref[span, :]
        q_halves, g_halves = _halves(q), _halves(g)
        q_stack = jnp.concatenate(q_halves, 0)
        g_stack = jnp.concatenate(g_halves, 0)
        starts = starts_ref[:, span]
        places = halo + b * block + lax.broadcasted_iota(jnp.int32, (1, block), 1)
        product = g.astype(F32).T * out_ref[:, span]
        deltas = [
            jnp.sum(product[h * HEAD_DIM : (h + 1) * HEAD_DIM], 0, keepdims=True) for h in range(2)
        ]
        lses = [lse_ref[0, h : h + 1, span] for h in range(2)]

        def step(c, carry):
            base = pl.multiple_of(c * KEYS, KEYS)
            here = pl.ds(base, KEYS)
            k_chunk = k_ref[here, :]
            v_chunk = v_ref[here, :]
            shares, scores, new = [], [], []
            for h in range(2):
                s = _scores(k_chunk, q_halves[h], base, starts, places)
                share = jnp.exp2(s - lses[h])
                grad_share = dot_nt(v_chunk, g_halves[h])
                grad_score = (share * (grad_share - deltas[h])).astype(BF)
                shares.append(share.astype(BF))
                scores.append(grad_score)
                kt = kt_ref[h * HEAD_DIM : (h + 1) * HEAD_DIM, here]
                new.append(carry[h] + dot_nn(kt, grad_score))
            gk_acc[here, :] += dot_nn(jnp.concatenate(scores, 1), q_stack)
            gv_acc[here, :] += dot_nn(jnp.concatenate(shares, 1), g_stack)
            return tuple(new)

        zero = jnp.zeros((HEAD_DIM, block), F32)
        last = -(-(halo + (b + 1) * block) // KEYS)
        got = lax.fori_loop(lows[b], last, step, (zero, zero))
        gq_ref[span, :] = (jnp.concatenate(got, 0).T * scale).astype(BF)
    gkv_ref[0] = (gk_acc[...] * scale).astype(BF)
    gkv_ref[1] = gv_acc[...].astype(BF)


def attend_backward(q, kv, grad_attended, out_t, lse, starts, lows):
    rows, window = q.shape[0], kv.shape[0]
    halo = window - rows
    pairs = q.shape[1] // 128

    def kernel(lows_ref, *refs):
        attend_backward_kernel(rows, halo, lows_ref, *refs)

    return pl.pallas_call(
        kernel,
        grid_spec=pltpu.PrefetchScalarGridSpec(
            num_scalar_prefetch=1,
            grid=(pairs,),
            in_specs=[
                pl.BlockSpec((rows, 128), lambda p, lows: (0, p)),
                pl.BlockSpec((window, 128), lambda p, lows: (0, p)),
                pl.BlockSpec((window, 128), lambda p, lows: (0, pairs + p)),
                pl.BlockSpec((rows, 128), lambda p, lows: (0, p)),
                pl.BlockSpec((128, rows), lambda p, lows: (p, 0)),
                pl.BlockSpec((1, 2, rows), lambda p, lows: (p, 0, 0)),
                pl.BlockSpec((1, rows), lambda p, lows: (0, 0)),
            ],
            out_specs=[
                pl.BlockSpec((rows, 128), lambda p, lows: (0, p)),
                pl.BlockSpec((2, window, 128), lambda p, lows: (0, 0, p)),
            ],
            scratch_shapes=[
                pltpu.VMEM((128, window), BF),
                pltpu.VMEM((window, 128), F32),
                pltpu.VMEM((window, 128), F32),
            ],
        ),
        out_shape=[
            jax.ShapeDtypeStruct(q.shape, BF),
            jax.ShapeDtypeStruct((2, window, q.shape[1]), BF),
        ],
        cost_estimate=pl.CostEstimate(
            flops=10 * rows * window * q.shape[1], bytes_accessed=24 << 20, transcendentals=0
        ),
        compiler_params=pltpu.CompilerParams(vmem_limit_bytes=40 << 20),
    )(lows, q, kv, kv, grad_attended, out_t, lse, starts)


def gather_matrix(shard):
    whole = lax.all_gather(shard.astype(BF), "tensor", axis=shard.ndim - 1, tiled=True)
    return lax.all_gather(whole, "dp", axis=0, tiled=True)


def scatter_matrix(grad):
    part = lax.psum_scatter(grad, "dp", scatter_dimension=0, tiled=True)
    return lax.psum_scatter(part, "tensor", scatter_dimension=grad.ndim - 1, tiled=True).astype(F32)


def from_before(value):
    n = lax.axis_size("tensor")
    return lax.ppermute(value, "tensor", [(i, i + 1) for i in range(n - 1)])


def to_before(value):
    n = lax.axis_size("tensor")
    return lax.ppermute(value, "tensor", [(i + 1, i) for i in range(n - 1)])


def body(
    tokens,
    out_grad,
    seq_lengths,
    master_qkv,
    first_qkv,
    second_qkv,
    master_mix,
    first_mix,
    second_mix,
    master_up,
    first_up,
    second_up,
    master_down,
    first_down,
    second_down,
    master_norms,
    first_norms,
    second_norms,
    master_midnorm,
    first_midnorm,
    second_midnorm,
    master_heads,
    first_heads,
    second_heads,
):
    parts = lax.axis_size("tensor")
    place = lax.axis_index("tensor")
    rows, model = tokens.shape
    hops = min(-(-(LONGEST - 1) // rows), parts - 1)
    halo = hops * rows
    block = min(256, rows)

    ends = jnp.cumsum(seq_lengths[0])
    places = place * rows + jnp.arange(rows, dtype=jnp.int32)
    begun = jnp.where(places[:, None] >= ends[None, :], ends[None, :], 0)
    starts = jnp.max(begun, 1).astype(jnp.int32) - place * rows + halo
    lows = starts[::block] // KEYS
    starts = starts[None, :]

    w_qkv = gather_matrix(master_qkv).reshape(model, 3 * model)
    w_mix = gather_matrix(master_mix)
    w_up = gather_matrix(master_up)
    w_down = gather_matrix(master_down)
    w_q, w_kv = w_qkv[:, :model], w_qkv[:, model:]

    inputs = tokens.astype(F32)
    normed_one, normal_one, scale_one = norm_forward(inputs, master_norms[0], master_norms[1])
    normed_one = normed_one.astype(BF)
    window = [normed_one]
    for _ in range(hops):
        window.insert(0, from_before(window[0]))
    window = jnp.concatenate(window, 0)
    queries = dot_nn(normed_one, w_q).astype(BF)
    keys_values = dot_nn(window, w_kv).astype(BF)
    out_t, lse = attend_forward(queries, keys_values, starts, lows)
    attended = out_t.T
    gains = jnp.repeat(master_heads, HEAD_DIM)
    scaled = (attended * gains[None, :]).astype(BF)
    mixed = dot_nt(scaled, w_mix)
    post, normal_two, scale_two = norm_forward(mixed, master_norms[2], master_norms[3])
    hidden = inputs + post
    normed_three, normal_three, scale_three = norm_forward(hidden, master_norms[4], master_norms[5])
    normed_three = normed_three.astype(BF)
    upper = dot_nn(normed_three, w_up)
    activated, gelu_back = jax.vjp(gelu_exact, upper)
    mean_row = jnp.sum(activated, 1, keepdims=True) / FF
    spread = jnp.sum(activated * activated, 1, keepdims=True) / FF - mean_row * mean_row
    scale_mid = lax.rsqrt(spread + eps_norm)
    normal_mid = (activated - mean_row) * scale_mid
    reshaped = (normal_mid * master_midnorm[0] + master_midnorm[1]).astype(BF)
    layer_out = (hidden + dot_nt(reshaped, w_down)).astype(BF)

    grad_down = dot_tn(out_grad, reshaped).astype(BF)
    shard_down = scatter_matrix(grad_down)
    grad_reshaped = dot_nn(out_grad, w_down)
    grad_normal_mid = grad_reshaped * master_midnorm[0]
    sum_one = jnp.sum(grad_normal_mid, 1, keepdims=True) / FF
    sum_two = jnp.sum(grad_normal_mid * normal_mid, 1, keepdims=True) / FF
    grad_activated = scale_mid * (grad_normal_mid - sum_one - normal_mid * sum_two)
    grad_upper = gelu_back(grad_activated)[0].astype(BF)
    grad_midnorm = jnp.stack([jnp.sum(grad_reshaped * normal_mid, 0), jnp.sum(grad_reshaped, 0)])
    grad_up = dot_tn(normed_three, grad_upper).astype(BF)
    shard_up = scatter_matrix(grad_up)
    grad_normed_three = dot_nt(grad_upper, w_up)
    grad_hidden_ffn, grad_gain_three, grad_bias_three = norm_backward(
        grad_normed_three, normal_three, scale_three, master_norms[4]
    )
    grad_hidden = out_grad.astype(F32) + grad_hidden_ffn
    grad_mixed, grad_gain_two, grad_bias_two = norm_backward(
        grad_hidden, normal_two, scale_two, master_norms[2]
    )
    grad_mixed = grad_mixed.astype(BF)
    grad_scaled = dot_nn(grad_mixed, w_mix)
    grad_mix = dot_tn(grad_mixed, scaled).astype(BF)
    shard_mix = scatter_matrix(grad_mix)
    grad_heads = jnp.sum((grad_scaled * attended).reshape(rows, HEADS, HEAD_DIM), (0, 2))
    grad_attended = (grad_scaled * gains[None, :]).astype(BF)
    grad_q, grad_kv = attend_backward(queries, keys_values, grad_attended, out_t, lse, starts, lows)
    grad_k, grad_v = grad_kv[0], grad_kv[1]
    grad_window = dot_nt(grad_k, w_kv[:, :model]) + dot_nt(grad_v, w_kv[:, model:])
    back = None
    for hop in range(hops):
        part = grad_window[hop * rows : (hop + 1) * rows]
        back = to_before((part if back is None else part + back).astype(BF)).astype(F32)
    grad_normed_one = grad_window[halo:] + dot_nt(grad_q, w_q)
    if back is not None:
        grad_normed_one = grad_normed_one + back
    grad_qkv = jnp.stack(
        [
            dot_tn(normed_one, grad_q).astype(BF),
            dot_tn(window, grad_k).astype(BF),
            dot_tn(window, grad_v).astype(BF),
        ],
        1,
    )
    shard_qkv = scatter_matrix(grad_qkv)
    grad_in, grad_gain_one, grad_bias_one = norm_backward(
        grad_normed_one, normal_one, scale_one, master_norms[0]
    )
    input_grad = grad_hidden + grad_in

    grad_norms = jnp.stack(
        [
            grad_gain_one,
            grad_bias_one,
            grad_gain_two,
            grad_bias_two,
            grad_gain_three,
            grad_bias_three,
        ]
    )
    grad_norms, grad_midnorm, grad_heads = lax.psum(
        (grad_norms, grad_midnorm, grad_heads), ("dp", "tensor")
    )
    new_qkv = adam_update(master_qkv, first_qkv, second_qkv, shard_qkv, rate_matrix, decay_matrix)
    new_mix = adam_update(master_mix, first_mix, second_mix, shard_mix, rate_matrix, decay_matrix)
    new_up = adam_update(master_up, first_up, second_up, shard_up, rate_matrix, decay_matrix)
    new_down = adam_update(
        master_down, first_down, second_down, shard_down, rate_matrix, decay_matrix
    )
    new_norms = adam_update(master_norms, first_norms, second_norms, grad_norms, rate_vector, 0.0)
    new_midnorm = adam_update(
        master_midnorm, first_midnorm, second_midnorm, grad_midnorm, rate_vector, 0.0
    )
    new_heads = adam_update(master_heads, first_heads, second_heads, grad_heads, rate_vector, 0.0)
    return (
        (layer_out, input_grad)
        + new_qkv
        + new_mix
        + new_up
        + new_down
        + new_norms
        + new_midnorm
        + new_heads
    )


def solution(mesh):
    token, matrix, cube = P(("dp", "tensor"), None), P("dp", "tensor"), P("dp", None, "tensor")
    in_specs = (token, token, P("dp", None)) + (cube,) * 3 + (matrix,) * 9 + (P(),) * 9
    out_specs = (token, token) + (cube,) * 3 + (matrix,) * 9 + (P(),) * 9
    return jax.shard_map(body, mesh=mesh, in_specs=in_specs, out_specs=out_specs, check_vma=False)
```
